768 devices in a mesh: node: 8 (over y_hi, x), span: 96 (over y_lo, z, core).
Axes of the slice: x: 4, y: 8 (y_hi: 2, y_lo: 4; y = y_hi * 4 + y_lo), z: 12, core: 2. Of those that a mesh axis runs over, the one named last changes fastest.
Arguments:
- iterate: float32 [8, 2, 576, 4608], P('node', None, None, 'span'), may hold values from -6 to 6
- start_field: float32 [2, 576, 4608], P(None, None, 'span'), may hold values from -6 to 6
- spanwise_velocity: float32 [8, 576, 4608], P('node', 'span'), may hold values from -6 to 6
- eigen_basis: float32 [576, 576], replicated, may hold values from -3 to 3
- inverse_basis: float32 [576, 576], replicated, may hold values from -3 to 3, as said below
- decay_rates: float32 [576], replicated, may hold values from 0.05 to 5
Outputs:
- updated: float32 [8, 2, 576, 4608], P('node', None, None, 'span')
The draws below stay inside these ranges and needn't reach their ends.
Inputs may be any that keep to these rules, and one draw needn't show every extreme that they name: inverse_basis is the inverse of eigen_basis up to float32 rounding.
All inputs are finite; a program needn't handle non-finite values.
Results may differ from the reference program's by a relative error of at most 0.00054.
Values may be sent and summed in bfloat16 or wider, within the bound.
A program may use at most 64 MiB of HBM per device.

```python
import math
import jax
import jax.numpy as jnp
from jax import lax

NY = 576
NZ = 4608
NODES = 8


def basis_pair(key):
    branch_key = jax.random.fold_in(key, 41)
    identity = jnp.eye(NY, dtype=jnp.float32)
    spread = 0.3 * jax.random.truncated_normal(branch_key, -3.0, 3.0, (NY, NY), jnp.float32)
    matrix = identity + spread / jnp.sqrt(jnp.float32(NY))
    inverse = jnp.linalg.solve(matrix, identity)
    return (matrix, inverse)


def draw_eigen_basis(key, part):
    return basis_pair(key)[0]


def draw_inverse_basis(key, part):
    return basis_pair(key)[1]


def block_scale(own_key, extent, shards, smallest, high):
    loudness = 1.0
    for position, shards_of in shards:
        steps = jax.random.uniform(jax.random.fold_in(jax.random.fold_in(own_key, 6), position), (shards_of,), jnp.float32, smallest / len(shards), high / len(shards))
        loudness = loudness * jnp.repeat(jnp.exp(steps), extent[position] // shards_of).reshape((-1,) + (1,) * (len(extent) - 1 - position))
    return loudness


def bell_draw(key, extent, width, limit, pieces=(), kind=jnp.bfloat16):
    entries = jax.random.normal(key, extent, jnp.float32) * width
    if len(pieces) > 0:
        entries = block_scale(key, extent, pieces, -0.22, 0.18) * entries
    return jnp.clip(entries, min=-limit, max=limit).astype(kind)


def setup_inputs(seed: int = 0) -> dict:
    splits = jax.random.split(jax.random.key(seed), 7)
    iterate = bell_draw(splits[0], (NODES, 2, NY, NZ), 1.0, 6.0, ((0, 8), (3, 96)), jnp.float32)
    start_field = bell_draw(splits[1], (2, NY, NZ), 1.0, 6.0, ((2, 96),), jnp.float32)
    spanwise_velocity = bell_draw(splits[2], (NODES, NY, NZ), 1.0, 6.0, ((0, 8), (1, 96)), jnp.float32)
    eigen_basis = draw_eigen_basis(jax.random.fold_in(splits[6], 71), 0)
    inverse_basis = draw_inverse_basis(jax.random.fold_in(splits[6], 71), 0)
    decay_rates = jnp.clip(jnp.exp(jax.random.uniform(splits[5], (NY,), jnp.float32, math.log(0.05), math.log(5.0))), 0.05, 5.0)
    return {"iterate": iterate, "start_field": start_field, "spanwise_velocity": spanwise_velocity, "eigen_basis": eigen_basis, "inverse_basis": inverse_basis, "decay_rates": decay_rates}


def collocation(node_total):
    points = [0.5 - 0.5 * math.cos((2.0 * m + 1.0) * math.pi / (2.0 * node_total)) for m in range(node_total)]
    weights = [[0.0] * node_total for _ in range(node_total)]
    for column in range(node_total):
        coeffs = [1.0]
        scale = 1.0
        for other in range(node_total):
            if other != column:
                grown = [0.0] * (len(coeffs) + 1)
                for power in range(len(coeffs)):
                    grown[power + 1] += coeffs[power]
                    grown[power] -= points[other] * coeffs[power]
                coeffs = grown
                scale = scale * (points[column] - points[other])
        for row in range(node_total):
            total = 0.0
            for power in range(len(coeffs)):
                total += coeffs[power] * points[row] ** (power + 1) / (power + 1)
            weights[row][column] = total / scale
    return (weights, [value / node_total for value in points])

def reference(iterate, start_field, spanwise_velocity, eigen_basis, inverse_basis, decay_rates):
    highest = lax.Precision.HIGHEST
    quadrature_table, shift_table = collocation(NODES)
    quadrature = jnp.asarray(quadrature_table, jnp.float32)
    shifts = jnp.asarray(shift_table, jnp.float32)
    wavenumber = jnp.arange(NZ, dtype=jnp.int32)
    signed = jnp.where(wavenumber < NZ // 2, wavenumber, wavenumber - NZ).astype(jnp.float32) / (NZ // 2)
    damping = decay_rates[:, None] + signed[None, :] ** 2
    gradient_real = lax.optimization_barrier((-signed * iterate[:, 1]).astype(jnp.bfloat16)).astype(jnp.float32)
    gradient_imaginary = lax.optimization_barrier((signed * iterate[:, 0]).astype(jnp.bfloat16)).astype(jnp.float32)
    physical = jnp.fft.ifft(lax.complex(gradient_real, gradient_imaginary), axis=-1, norm='ortho')
    spectral = jnp.fft.fft(-spanwise_velocity * physical, axis=-1, norm='ortho')
    advect = jnp.stack([jnp.real(spectral), jnp.imag(spectral)], axis=1)
    advect = lax.optimization_barrier(advect.astype(jnp.bfloat16)).astype(jnp.float32)
    coefficients = jnp.einsum('yx,mcxq->mcyq', inverse_basis, iterate, precision=highest)
    start_coeff = jnp.einsum('yx,cxq->cyq', inverse_basis, start_field, precision=highest)
    section_term = -damping * coefficients + jnp.einsum('yx,mcxq->mcyq', inverse_basis, advect, precision=highest)
    summed = jnp.einsum('mj,jcyq->mcyq', quadrature, section_term, precision=highest)
    node_shift = shifts[:, None, None, None] * damping
    new_coeff = (start_coeff[None] + summed + node_shift * coefficients) / (1.0 + node_shift)
    return jnp.einsum('yx,mcxq->mcyq', eigen_basis, new_coeff, precision=highest)
```

```python
import functools
import math

import jax
import jax.numpy as jnp
import ml_dtypes
import numpy as np
from jax import lax
from jax.experimental import pallas as pl
from jax.experimental.pallas import tpu as pltpu
from jax.sharding import PartitionSpec as P

MESH = pl.DeviceIdType.MESH
BF = jnp.bfloat16
F32 = jnp.float32
HALF = 64
LANES = 128


def collocation(node_total):
    points = [
        0.5 - 0.5 * math.cos((2.0 * m + 1.0) * math.pi / (2.0 * node_total))
        for m in range(node_total)
    ]
    weights = [[0.0] * node_total for _ in range(node_total)]
    for column in range(node_total):
        coeffs = [1.0]
        scale = 1.0
        for other in range(node_total):
            if other != column:
                grown = [0.0] * (len(coeffs) + 1)
                for power in range(len(coeffs)):
                    grown[power + 1] += coeffs[power]
                    grown[power] -= points[other] * coeffs[power]
                coeffs = grown
                scale = scale * (points[column] - points[other])
        for row in range(node_total):
            total = 0.0
            for power in range(len(coeffs)):
                total += coeffs[power] * points[row] ** (power + 1) / (power + 1)
            weights[row][column] = total / scale
    return (weights, [value / node_total for value in points])


def split_np(table):
    high = table.astype(np.float32).astype(ml_dtypes.bfloat16)
    low = (table - high.astype(np.float64)).astype(ml_dtypes.bfloat16)
    return high, low


def tables(span, local_modes, lines):
    nz = span * local_modes
    s = np.arange(span, dtype=np.int64)
    r = np.arange(local_modes, dtype=np.int64)
    outer = 2 * np.pi * ((s[:, None] * s[None, :]) % span) / span
    inner = 2 * np.pi * ((r[:, None] * r[None, :]) % local_modes) / local_modes
    twist = 2 * np.pi * (s[:, None] * r[None, :]) / nz
    first = np.zeros((LANES, 2 * span))
    first[:span, :span] = np.cos(outer)
    first[:span, span:] = np.sin(outer)
    last = np.zeros((LANES, 2 * LANES))
    last[:span, :span] = np.cos(outer)
    last[:span, LANES : LANES + span] = np.sin(outer)

    def complex_block(phase):
        block = np.zeros((LANES, LANES))
        n = local_modes
        block[:n, :n] = np.cos(phase)
        block[:n, HALF : HALF + n] = -np.sin(phase)
        block[HALF : HALF + n, :n] = np.sin(phase)
        block[HALF : HALF + n, HALF : HALF + n] = np.cos(phase)
        return block

    to_points = complex_block(inner)
    to_modes = complex_block(-inner)
    cosine, sine = np.zeros((LANES, LANES)), np.zeros((LANES, LANES))
    cosine[:span, :local_modes] = np.cos(twist)
    cosine[:span, HALF : HALF + local_modes] = np.cos(twist)
    sine[:span, :local_modes] = -np.sin(twist)
    sine[:span, HALF : HALF + local_modes] = np.sin(twist)
    turns = np.concatenate([cosine, sine, cosine.T, -sine.T], axis=1).astype(np.float32)
    group = math.gcd(16, span)
    spread = np.zeros((LANES, 2 * LANES))
    for g in range(group):
        for y in range(lines):
            spread[g * 8 + y, g * lines + y] = 1.0
            spread[g * lines + y, LANES + g * 8 + y] = 1.0
    width = 2 * LANES

    def wide(a):
        out = np.zeros((LANES, width), ml_dtypes.bfloat16)
        out[:, : a.shape[1]] = a
        return out

    parts = []
    for table in (first, last):
        parts += [wide(t) for t in split_np(table)]
    for table in (to_points, to_modes):
        parts.append(np.concatenate(split_np(table), axis=1))
    parts.append(wide(spread.astype(ml_dtypes.bfloat16)))
    return np.concatenate(parts, axis=0), turns


def dot(a, b):
    return jnp.dot(a, b, preferred_element_type=F32)


def dot_t(a, b):
    return lax.dot_general(a, b, (((1,), (1,)), ((), ())), preferred_element_type=F32)


def split(x):
    high = x.astype(BF)
    return high, (x - high.astype(F32)).astype(BF)


def three(product, a, b):
    return product(a[0], b[0]) + (product(a[0], b[1]) + product(a[1], b[0]))


def side_by_side(pair_ref, local_modes):
    rows = pair_ref.shape[1]
    gap = jnp.zeros((rows, HALF - local_modes), F32)
    return jnp.concatenate([pair_ref[0], gap, pair_ref[1], gap], axis=1)


def turned(x):
    return pltpu.roll(x, HALF, axis=1)


def sweep(
    nodes, span, lines, quadrature, shifts,
    it_ref, st_ref, vel_ref, eig_ref, inv_ref, rate_ref, mats_ref, turns_ref,
    out_ref,
    fields, inv_hi, inv_lo, eig_hi, eig_lo, velocity, coeff, base, inverse_den,
    lines_f32, e1_out, e1_in, r_in, r_out, r_all, e2_out, e2_in, a_out, a_all,
    e1_send, e1_recv, rt_send, rt_recv, rb_send, rb_recv,
    e2_send, e2_own, e2_recv, ab_send, ab_recv,
):
    ny, local_modes = it_ref.shape[1], it_ref.shape[2]
    share = span // nodes
    rows = ny // nodes
    node, me = lax.axis_index("node"), lax.axis_index("span")
    nz = span * local_modes

    barrier = pltpu.get_barrier_semaphore()

    def greet(k, carry):
        pl.semaphore_signal(
            barrier, 1, device_id={"span": lax.rem(me + k, span)}, device_id_type=MESH
        )
        return carry

    lax.fori_loop(1, span, greet, 0)
    for k in range(1, nodes):
        pl.semaphore_signal(
            barrier, 1, device_id={"node": lax.rem(node + k, nodes)}, device_id_type=MESH
        )

    lane = lax.broadcasted_iota(jnp.int32, (1, LANES), 1)
    mode = me * local_modes + lax.rem(lane, HALF)
    signed = jnp.where(mode < nz // 2, mode, mode - nz).astype(F32) / (nz // 2)
    turn_sign = jnp.where(lane < HALF, -1.0, 1.0).astype(F32)
    fields[...] = side_by_side(it_ref, local_modes)
    gradient = (turned(fields[...]) * (signed * turn_sign)).astype(BF)
    group = math.gcd(16, span)
    spread = mats_ref[pl.ds(6 * LANES, group * 8), : group * lines]
    gather = mats_ref[pl.ds(6 * LANES, group * lines), LANES : LANES + group * 8]
    for g in range(span // group):
        block = dot(spread, gradient[g * group * lines : (g + 1) * group * lines])
        e1_out[pl.ds(g * group, group)] = block.reshape(group, 8, LANES).astype(BF)
    high, low = split(inv_ref[...])
    inv_hi[...] = high
    inv_lo[...] = low
    high, low = split(eig_ref[...])
    eig_hi[...] = high
    eig_lo[...] = low
    inverse = (inv_hi, inv_lo)

    def by_inverse(x):
        return three(dot, (inv_hi[...], inv_lo[...]), split(x))

    start = side_by_side(st_ref, local_modes)
    coeff[...] = by_inverse(jnp.concatenate([fields[...], start], axis=1))
    velocity[...] = jnp.zeros_like(velocity)
    for y in range(lines):
        part = vel_ref[y] * (-1.0 / nz)
        velocity[0:local_modes, y * LANES : y * LANES + span] = part
        velocity[HALF : HALF + local_modes, y * LANES : y * LANES + span] = part
    lines_f32[...] = jnp.zeros_like(lines_f32)

    pl.semaphore_wait(barrier, span - 1 + nodes - 1)

    def send_lines(k, carry):
        peer = lax.rem(me + k, span)
        pltpu.make_async_remote_copy(
            src_ref=e1_out.at[peer], dst_ref=e1_in.at[me], send_sem=e1_send, recv_sem=e1_recv,
            device_id={"span": peer}, device_id_type=MESH,
        ).start()
        return carry

    lax.fori_loop(1, span, send_lines, 0)

    def node_copies(source, target, send_sem, recv_sem):
        out = []
        for k in range(1, nodes):
            peer = lax.rem(node + k, nodes)
            out.append(
                pltpu.make_async_remote_copy(
                    src_ref=source(peer), dst_ref=target, send_sem=send_sem, recv_sem=recv_sem,
                    device_id={"node": peer}, device_id_type=MESH,
                )
            )
        for copy in out:
            copy.start()

    node_copies(
        lambda peer: fields.at[pl.ds(pl.multiple_of(peer * rows, 8), rows)],
        r_in.at[node], rt_send, rt_recv,
    )
    e1_in[me] = e1_out[me]
    r_in[node] = fields[pl.ds(pl.multiple_of(node * rows, 8), rows)]
    some = pl.ds(0, nodes - 1)
    pltpu.make_async_copy(r_in.at[some], r_out.at[some], rt_recv).wait()

    def blend_fields(i, carry):
        at = pl.ds(pl.multiple_of(i * 8, 8), 8)
        terms = [r_in[j, at] for j in range(nodes)]
        for m in range(nodes):
            total = terms[0] * quadrature[m][0]
            for j in range(1, nodes):
                total = total + terms[j] * quadrature[m][j]
            r_out[m, at] = total
        return carry

    lax.fori_loop(0, rows // 8, blend_fields, 0)
    node_copies(lambda peer: r_out.at[peer], r_all.at[node], rb_send, rb_recv)
    r_all[node] = r_out[node]

    most = pl.ds(0, span - 1)
    pltpu.make_async_copy(e1_out.at[most], e1_in.at[most], e1_recv).wait()

    lines_f32[...] = e1_in[...].astype(F32)
    columns = [lines_f32[:, y, :] for y in range(lines)]
    stacked = jnp.concatenate(
        [
            jnp.concatenate(columns, axis=1),
            jnp.concatenate([turned(c) * turn_sign for c in columns], axis=1),
        ],
        axis=0,
    ).astype(BF)
    two = pl.ds(0, LANES)
    first_hi = mats_ref[pl.ds(0, LANES), : 2 * span]
    first_lo = mats_ref[pl.ds(LANES, LANES), : 2 * span]
    grid = dot(first_hi, stacked) + dot(first_lo, stacked)
    cosine, sine = turns_ref[:, 0:LANES], turns_ref[:, LANES : 2 * LANES]
    pieces = []
    for y in range(lines):
        piece = grid[:, y * LANES : (y + 1) * LANES]
        pieces.append(piece * cosine + turned(piece) * sine)
    tall = split(jnp.concatenate(pieces, axis=0))
    to_points = [mats_ref[pl.ds(4 * LANES, LANES), i * LANES : (i + 1) * LANES] for i in (0, 1)]
    to_modes = [mats_ref[pl.ds(5 * LANES, LANES), i * LANES : (i + 1) * LANES] for i in (0, 1)]
    physical = three(dot_t, to_points, tall)
    modes = three(dot, to_modes, split(physical * velocity[...]))
    swapped = jnp.concatenate([modes[HALF:], modes[:HALF]], axis=0)
    cosine, sine = turns_ref[:, 2 * LANES : 3 * LANES], turns_ref[:, 3 * LANES : 4 * LANES]
    pieces = []
    for y in range(lines):
        at = slice(y * LANES, (y + 1) * LANES)
        piece = modes[:, at] * cosine + swapped[:, at] * sine
        other = jnp.concatenate([piece[HALF:], -piece[:HALF]], axis=0)
        pieces.append(jnp.concatenate([piece, other], axis=1))
    tall = split(jnp.concatenate(pieces, axis=0))
    last = [mats_ref[pl.ds(i * LANES, span), :] for i in (2, 3)]
    spectral = three(dot_t, last, tall)
    for y in range(lines):
        lines_f32[:, y, :] = spectral[:, y * LANES : (y + 1) * LANES]
    e2_out[...] = lines_f32[...].astype(BF)

    combiner = me // share
    slot = node * share + lax.rem(me, share)

    def send_modes(k, carry):
        peer = lax.rem(me + k, span)
        pltpu.make_async_remote_copy(
            src_ref=e2_out.at[peer], dst_ref=e2_in.at[slot], send_sem=e2_send, recv_sem=e2_recv,
            device_id={"node": combiner, "span": peer}, device_id_type=MESH,
        ).start()
        return carry

    lax.fori_loop(1, span, send_modes, 0)
    own = pltpu.make_async_remote_copy(
        src_ref=e2_out.at[me], dst_ref=e2_in.at[slot], send_sem=e2_own, recv_sem=e2_recv,
        device_id={"node": combiner}, device_id_type=MESH,
    )

    @pl.when(combiner != node)
    def _():
        own.start()

    @pl.when(combiner == node)
    def _():
        pltpu.make_async_copy(e2_out.at[me], e2_in.at[slot], e2_recv).start()

    pltpu.make_async_copy(r_out.at[some], r_all.at[some], rb_recv).wait()
    shift = jnp.float32(0.0)
    for m in range(nodes):
        shift = jnp.where(node == m, jnp.float32(shifts[m]), shift)
    damping = rate_ref[...] + signed * signed
    weighted = by_inverse(r_all[...].reshape(ny, LANES))
    inverse_den[...] = 1.0 / (1.0 + shift * damping)
    known = coeff[:, LANES:] - damping * weighted + (shift * damping) * coeff[:, :LANES]
    base[...] = three(
        dot, (eig_hi[...], eig_lo[...]), split(known * inverse_den[...])
    )

    pltpu.make_async_copy(e2_out, e2_in, e2_recv).wait()

    def blend_modes(i, carry):
        terms = [e2_in[j * share + i].astype(F32) for j in range(nodes)]
        for m in range(nodes):
            total = terms[0] * quadrature[m][0]
            for j in range(1, nodes):
                total = total + terms[j] * quadrature[m][j]
            a_out[m, i] = total.astype(BF)
        return carry

    lax.fori_loop(0, share, blend_modes, 0)
    node_copies(lambda peer: a_out.at[peer], a_all.at[node], ab_send, ab_recv)
    a_all[node] = a_out[node]
    pltpu.make_async_copy(a_out.at[some], a_all.at[some], ab_recv).wait()
    arrived = a_all[...].astype(F32).reshape(span * 8, LANES).astype(BF)
    terms = []
    for g in range(span // group):
        terms.append(dot(gather, arrived[g * group * 8 : (g + 1) * group * 8]))
    term = jnp.concatenate(terms, axis=0).astype(BF)
    projected = dot(inv_hi[...], term) + dot(inv_lo[...], term)
    result = base[...] + three(
        dot, (eig_hi[...], eig_lo[...]), split(projected * inverse_den[...])
    )
    out_ref[0] = result[:, :local_modes]
    out_ref[1] = result[:, HALF : HALF + local_modes]

    pltpu.make_async_copy(e1_out.at[most], e1_in.at[most], e1_send).wait()
    pltpu.make_async_copy(r_in.at[some], r_out.at[some], rt_send).wait()
    pltpu.make_async_copy(r_out.at[some], r_all.at[some], rb_send).wait()
    pltpu.make_async_copy(e2_out.at[most], e2_in.at[most], e2_send).wait()
    pltpu.make_async_copy(a_out.at[some], a_all.at[some], ab_send).wait()

    @pl.when(combiner != node)
    def _():
        own.wait_send()


def local(nodes, span, iterate, start_field, spanwise_velocity, eigen_basis, inverse_basis, decay_rates):
    ny, local_modes = iterate.shape[2], iterate.shape[3]
    lines = spanwise_velocity.shape[1]
    share, rows = span // nodes, ny // nodes
    quadrature, shifts = collocation(nodes)
    mats, turns = tables(span, local_modes, lines)
    velocity = spanwise_velocity[0].reshape(lines, local_modes, span)
    vmem = pl.BlockSpec(memory_space=pltpu.VMEM)
    sem = pltpu.SemaphoreType.DMA
    return pl.pallas_call(
        functools.partial(sweep, nodes, span, lines, quadrature, shifts),
        out_shape=jax.ShapeDtypeStruct((2, ny, local_modes), F32),
        in_specs=[vmem] * 8,
        out_specs=vmem,
        scratch_shapes=[
            pltpu.VMEM((ny, LANES), F32),
            pltpu.VMEM((ny, ny), BF),
            pltpu.VMEM((ny, ny), BF),
            pltpu.VMEM((ny, ny), BF),
            pltpu.VMEM((ny, ny), BF),
            pltpu.VMEM((LANES, lines * LANES), F32),
            pltpu.VMEM((ny, 2 * LANES), F32),
            pltpu.VMEM((ny, LANES), F32),
            pltpu.VMEM((ny, LANES), F32),
            pltpu.VMEM((span, 8, LANES), F32),
            pltpu.VMEM((span, 8, LANES), BF),
            pltpu.VMEM((span, 8, LANES), BF),
            pltpu.VMEM((nodes, rows, LANES), F32),
            pltpu.VMEM((nodes, rows, LANES), F32),
            pltpu.VMEM((nodes, rows, LANES), F32),
            pltpu.VMEM((span, 8, LANES), BF),
            pltpu.VMEM((span, 8, LANES), BF),
            pltpu.VMEM((nodes, share, 8, LANES), BF),
            pltpu.VMEM((nodes, share, 8, LANES), BF),
        ]
        + [sem] * 11,
        compiler_params=pltpu.CompilerParams(
            collective_id=0, has_side_effects=True, vmem_limit_bytes=40 << 20
        ),
    )(
        iterate[0], start_field, velocity, eigen_basis, inverse_basis,
        decay_rates[:, None], jnp.asarray(mats), jnp.asarray(turns),
    )[None]


def solution(mesh):
    return jax.shard_map(
        functools.partial(local, mesh.shape["node"], mesh.shape["span"]),
        mesh=mesh,
        in_specs=(
            P("node", None, None, "span"),
            P(None, None, "span"),
            P("node", "span", None),
            P(),
            P(),
            P(),
        ),
        out_specs=P("node", None, None, "span"),
        check_vma=False,
    )
```

```python
import functools
import math
from types import SimpleNamespace

import jax
import jax.numpy as jnp
import ml_dtypes
import numpy as np
from jax import lax
from jax.experimental import pallas as pl
from jax.experimental.pallas import tpu as pltpu
from jax.sharding import PartitionSpec as P

MESH = pl.DeviceIdType.MESH
BF = jnp.bfloat16
F32 = jnp.float32
HALF = 64
LANES = 128


def collocation(node_total):
    points = [
        0.5 - 0.5 * math.cos((2.0 * m + 1.0) * math.pi / (2.0 * node_total))
        for m in range(node_total)
    ]
    weights = [[0.0] * node_total for _ in range(node_total)]
    for column in range(node_total):
        coeffs = [1.0]
        scale = 1.0
        for other in range(node_total):
            if other != column:
                grown = [0.0] * (len(coeffs) + 1)
                for power in range(len(coeffs)):
                    grown[power + 1] += coeffs[power]
                    grown[power] -= points[other] * coeffs[power]
                coeffs = grown
                scale = scale * (points[column] - points[other])
        for row in range(node_total):
            total = 0.0
            for power in range(len(coeffs)):
                total += coeffs[power] * points[row] ** (power + 1) / (power + 1)
            weights[row][column] = total / scale
    return (weights, [value / node_total for value in points])


def split_np(table):
    high = table.astype(np.float32).astype(ml_dtypes.bfloat16)
    low = (table - high.astype(np.float64)).astype(ml_dtypes.bfloat16)
    return high, low


def tables(span, local_modes, lines):
    nz = span * local_modes
    s = np.arange(span, dtype=np.int64)
    r = np.arange(local_modes, dtype=np.int64)
    outer = 2 * np.pi * ((s[:, None] * s[None, :]) % span) / span
    inner = 2 * np.pi * ((r[:, None] * r[None, :]) % local_modes) / local_modes
    twist = 2 * np.pi * (s[:, None] * r[None, :]) / nz
    first = np.zeros((LANES, 2 * span))
    first[:span, :span] = np.cos(outer)
    first[:span, span:] = np.sin(outer)
    last = np.zeros((LANES, 2 * LANES))
    last[:span, :span] = np.cos(outer)
    last[:span, LANES : LANES + span] = np.sin(outer)

    place = (r % 4) * (HALF // 4) + r // 4

    def complex_block(phase, rows, columns):
        block = np.zeros((LANES, LANES))
        for i, row_half in enumerate((0, HALF)):
            for j, column_half in enumerate((0, HALF)):
                value = np.cos(phase) if i == j else (np.sin(phase) if i else -np.sin(phase))
                block[np.ix_(rows + row_half, columns + column_half)] = value
        return block

    to_points = complex_block(inner.T, place, r)
    to_modes = complex_block(-inner, r, place)
    cosine, sine = np.zeros((LANES, LANES)), np.zeros((LANES, LANES))
    cosine[:span, :local_modes] = np.cos(twist)
    cosine[:span, HALF : HALF + local_modes] = np.cos(twist)
    sine[:span, :local_modes] = -np.sin(twist)
    sine[:span, HALF : HALF + local_modes] = np.sin(twist)
    turns = np.concatenate([cosine, sine, cosine.T, -sine.T], axis=1).astype(np.float32)
    group = math.gcd(16, span)
    spread = np.zeros((LANES, 2 * LANES))
    for g in range(group):
        for y in range(lines):
            spread[g * 8 + y, g * lines + y] = 1.0
            spread[g * lines + y, LANES + g * 8 + y] = 1.0
    width = 2 * LANES

    def wide(a):
        out = np.zeros((LANES, width), ml_dtypes.bfloat16)
        out[:, : a.shape[1]] = a
        return out

    parts = []
    for table in (first, last):
        parts += [wide(t) for t in split_np(table)]
    for table in (to_points, to_modes):
        parts.append(np.concatenate(split_np(table), axis=1))
    parts.append(wide(spread.astype(ml_dtypes.bfloat16)))
    return np.concatenate(parts, axis=0), turns


def dot(a, b):
    return jnp.dot(a, b, preferred_element_type=F32)


def dot_t(a, b):
    return lax.dot_general(a, b, (((1,), (1,)), ((), ())), preferred_element_type=F32)


def split(x):
    high = x.astype(BF)
    return high, (x - high.astype(F32)).astype(BF)


def three(product, a, b):
    return product(a[0], b[0]) + (product(a[0], b[1]) + product(a[1], b[0]))


def turned(x):
    return pltpu.roll(x, HALF, axis=1)


def greet(barrier, where):
    pl.semaphore_signal(barrier, 1, device_id=where, device_id_type=MESH)


def greeted(barrier, count):
    pl.semaphore_wait(barrier, count)


def remote(source, target, send_sem, recv_sem, where):
    return pltpu.make_async_remote_copy(
        src_ref=source, dst_ref=target, send_sem=send_sem, recv_sem=recv_sem,
        device_id=where, device_id_type=MESH,
    )


def start(copy):
    copy.start()


def settle(source, target, sem):
    pltpu.make_async_copy(source, target, sem).wait()


def prepare_lines(c, v):
    v.fields_t[...] = jnp.zeros_like(v.fields_t)
    v.fields_t[0 : c.modes] = v.iterate[0]
    v.fields_t[HALF : HALF + c.modes] = v.iterate[1]
    v.fields[...] = v.fields_t[...].T
    gradient = (turned(v.fields[...]) * (c.signed * c.turn_sign)).astype(BF)
    spread = v.mats[pl.ds(6 * LANES, c.group * 8), : c.group * c.lines]
    for g in range(c.span // c.group):
        step = c.group * c.lines
        block = dot(spread, gradient[g * step : (g + 1) * step])
        v.e1_out[pl.ds(g * c.group, c.group)] = block.reshape(c.group, 8, LANES).astype(BF)


def prepare_rest(c, v):
    v.fields_t[0 : c.modes] = v.start_field[0]
    v.fields_t[HALF : HALF + c.modes] = v.start_field[1]
    high, low = split(v.inv[...])
    v.inv_hi[...] = high
    v.inv_lo[...] = low
    high, low = split(v.eig[...])
    v.eig_hi[...] = high
    v.eig_lo[...] = low
    both = jnp.concatenate([v.fields[...], v.fields_t[...].T], axis=1)
    v.coeff[...] = three(dot, (v.inv_hi[...], v.inv_lo[...]), split(both))
    v.damping[...] = jnp.broadcast_to(v.rate[...], (LANES, c.ny)).T + c.signed * c.signed
    v.velocity[...] = jnp.zeros_like(v.velocity)
    for y in range(c.lines):
        for k, part in enumerate(velocity_rows(c, v, y)):
            part = part * (-1.0 / c.nz)
            for half in (0, HALF):
                at = half + k * c.chunk_rows
                v.velocity[at : at + part.shape[0], y * LANES : (y + 1) * LANES] = part
    v.lines_f32[...] = jnp.zeros_like(v.lines_f32)


def velocity_rows(c, v, y):
    count = c.modes // 4
    rows = [v.velocity_in[pl.ds(y * count * 3 + i, count, stride=3), :] for i in range(3)]
    lane = lax.broadcasted_iota(jnp.int32, (1, LANES), 1)

    def rolled(i, by):
        return pltpu.roll(rows[i], by, axis=1)

    return (
        rows[0],
        jnp.where(lane < 32, rolled(0, 32), rolled(1, 32)),
        jnp.where(lane < 64, rolled(1, 64), rolled(2, 64)),
        rolled(2, 96),
    )


def mix(c, terms, m):
    total = terms[0] * c.quadrature[m][0]
    for j in range(1, c.nodes):
        total = total + terms[j] * c.quadrature[m][j]
    return total


def blend_fields(c, v):
    def step(i, carry):
        at = pl.ds(pl.multiple_of(i * 8, 8), 8)
        terms = [v.r_in[j, at] for j in range(c.nodes)]
        for m in range(c.nodes):
            v.r_out[m, at] = mix(c, terms, m)
        return carry

    lax.fori_loop(0, c.rows // 8, step, 0)


def blend_modes(c, v):
    def step(i, carry):
        terms = [v.e2_in[j * c.share + i].astype(F32) for j in range(c.nodes)]
        for m in range(c.nodes):
            v.a_out[m, i] = mix(c, terms, m).astype(BF)
        return carry

    lax.fori_loop(0, c.share, step, 0)


def transform(c, v):
    v.lines_f32[...] = v.e1_in[...].astype(F32)
    columns = [v.lines_f32[:, y, :] for y in range(c.lines)]
    stacked = jnp.concatenate(
        [
            jnp.concatenate(columns, axis=1),
            jnp.concatenate([turned(x) * c.turn_sign for x in columns], axis=1),
        ],
        axis=0,
    ).astype(BF)
    first = [v.mats[pl.ds(i * LANES, LANES), : 2 * c.span] for i in (0, 1)]
    grid = dot(first[0], stacked) + dot(first[1], stacked)
    cosine, sine = v.turns[:, 0:LANES], v.turns[:, LANES : 2 * LANES]
    pieces = []
    for y in range(c.lines):
        piece = grid[:, y * LANES : (y + 1) * LANES]
        pieces.append(piece * cosine + turned(piece) * sine)
    tall = split(jnp.concatenate(pieces, axis=0))
    to_points = [v.mats[pl.ds(4 * LANES, LANES), i * LANES : (i + 1) * LANES] for i in (0, 1)]
    to_modes = [v.mats[pl.ds(5 * LANES, LANES), i * LANES : (i + 1) * LANES] for i in (0, 1)]
    physical = three(dot_t, to_points, tall)
    modes = three(dot, to_modes, split(physical * v.velocity[...]))
    swapped = jnp.concatenate([modes[HALF:], modes[:HALF]], axis=0)
    cosine, sine = v.turns[:, 2 * LANES : 3 * LANES], v.turns[:, 3 * LANES : 4 * LANES]
    pieces = []
    for y in range(c.lines):
        at = slice(y * LANES, (y + 1) * LANES)
        piece = modes[:, at] * cosine + swapped[:, at] * sine
        other = jnp.concatenate([piece[HALF:], -piece[:HALF]], axis=0)
        pieces.append(jnp.concatenate([piece, other], axis=1))
    tall = split(jnp.concatenate(pieces, axis=0))
    last = [v.mats[pl.ds(i * LANES, c.span), :] for i in (2, 3)]
    spectral = three(dot_t, last, tall)
    for y in range(c.lines):
        v.lines_f32[:, y, :] = spectral[:, y * LANES : (y + 1) * LANES]
    v.e2_out[...] = v.lines_f32[...].astype(BF)


def known_part(c, v):
    weighted = three(
        dot, (v.inv_hi[...], v.inv_lo[...]), split(v.r_all[...].reshape(c.ny, LANES))
    )
    damping = v.damping[...]
    v.inverse_den[...] = 1.0 / (1.0 + c.shift * damping)
    known = v.coeff[:, LANES:] - damping * weighted + (c.shift * damping) * v.coeff[:, :LANES]
    v.base[...] = three(dot, (v.eig_hi[...], v.eig_lo[...]), split(known * v.inverse_den[...]))


def finish(c, v, out_ref):
    gather = v.mats[pl.ds(6 * LANES, c.group * c.lines), LANES : LANES + c.group * 8]
    arrived = v.a_all[...].astype(F32).reshape(c.span * 8, LANES).astype(BF)
    terms = []
    for g in range(c.span // c.group):
        terms.append(dot(gather, arrived[g * c.group * 8 : (g + 1) * c.group * 8]))
    term = jnp.concatenate(terms, axis=0).astype(BF)
    projected = dot(v.inv_hi[...], term) + dot(v.inv_lo[...], term)
    result = v.base[...] + three(
        dot, (v.eig_hi[...], v.eig_lo[...]), split(projected * v.inverse_den[...])
    )
    result = result.T
    out_ref[0] = result[0 : c.modes]
    out_ref[1] = result[HALF : HALF + c.modes]


INPUTS = ("iterate", "start_field", "velocity_in", "eig", "inv", "rate", "mats", "turns")


def sweep(sizes, names, *refs):
    c = SimpleNamespace(**sizes)
    count = len(INPUTS)
    sources, out_ref = refs[:count], refs[count]
    v = SimpleNamespace(**dict(zip(names, refs[count + 1 :], strict=True)))
    nodes, span = c.nodes, c.span
    node, me = lax.axis_index("node"), lax.axis_index("span")

    barrier = pltpu.get_barrier_semaphore()

    def greet_span(k, carry):
        greet(barrier, {"span": lax.rem(me + k, span)})
        return carry

    lax.fori_loop(1, span, greet_span, 0)
    for k in range(1, nodes):
        greet(barrier, {"node": lax.rem(node + k, nodes)})

    loads = {
        name: pltpu.make_async_copy(source, getattr(v, name), v.load.at[i])
        for i, (name, source) in enumerate(zip(INPUTS, sources, strict=True))
    }
    order = ("iterate", "mats", "inv", "start_field", "eig", "velocity_in", "rate", "turns")
    for name in order:
        loads[name].start()

    lane = lax.broadcasted_iota(jnp.int32, (1, LANES), 1)
    mode = me * c.modes + lax.rem(lane, HALF)
    c.signed = jnp.where(mode < c.nz // 2, mode, mode - c.nz).astype(F32) / (c.nz // 2)
    c.turn_sign = jnp.where(lane < HALF, -1.0, 1.0).astype(F32)
    c.shift = jnp.float32(0.0)
    for m in range(nodes):
        c.shift = jnp.where(node == m, jnp.float32(c.shifts[m]), c.shift)
    for name in order[:2]:
        loads[name].wait()
    prepare_lines(c, v)
    for name in order[2:]:
        loads[name].wait()
    prepare_rest(c, v)
    greeted(barrier, span - 1 + nodes - 1)

    def send_lines(k, carry):
        peer = lax.rem(me + k, span)
        start(remote(v.e1_out.at[peer], v.e1_in.at[me], v.e1_send, v.e1_recv, {"span": peer}))
        return carry

    lax.fori_loop(1, span, send_lines, 0)

    def to_nodes(source, target, send_sem, recv_sem):
        for k in range(1, nodes):
            peer = lax.rem(node + k, nodes)
            start(remote(source(peer), target, send_sem, recv_sem, {"node": peer}))

    def part(owner):
        return pl.ds(pl.multiple_of(owner * c.rows, 8), c.rows)

    to_nodes(lambda peer: v.fields.at[part(peer)], v.r_in.at[node], v.rt_send, v.rt_recv)
    v.e1_in[me] = v.e1_out[me]
    v.r_in[node] = v.fields[part(node)]
    some, most = pl.ds(0, nodes - 1), pl.ds(0, span - 1)
    settle(v.r_in.at[some], v.r_out.at[some], v.rt_recv)
    blend_fields(c, v)
    to_nodes(lambda peer: v.r_out.at[peer], v.r_all.at[node], v.rb_send, v.rb_recv)
    v.r_all[node] = v.r_out[node]

    settle(v.e1_out.at[most], v.e1_in.at[most], v.e1_recv)
    transform(c, v)

    combiner = me // c.share
    slot = node * c.share + lax.rem(me, c.share)

    def send_modes(k, carry):
        peer = lax.rem(me + k, span)
        where = {"node": combiner, "span": peer}
        start(remote(v.e2_out.at[peer], v.e2_in.at[slot], v.e2_send, v.e2_recv, where))
        return carry

    lax.fori_loop(1, span, send_modes, 0)
    own = remote(v.e2_out.at[me], v.e2_in.at[slot], v.e2_own, v.e2_recv, {"node": combiner})

    @pl.when(combiner != node)
    def _():
        start(own)

    @pl.when(combiner == node)
    def _():
        start(pltpu.make_async_copy(v.e2_out.at[me], v.e2_in.at[slot], v.e2_recv))

    settle(v.r_out.at[some], v.r_all.at[some], v.rb_recv)
    known_part(c, v)

    settle(v.e2_out, v.e2_in, v.e2_recv)
    blend_modes(c, v)
    to_nodes(lambda peer: v.a_out.at[peer], v.a_all.at[node], v.ab_send, v.ab_recv)
    v.a_all[node] = v.a_out[node]
    settle(v.a_out.at[some], v.a_all.at[some], v.ab_recv)
    finish(c, v, out_ref)

    settle(v.e1_out.at[most], v.e1_in.at[most], v.e1_send)
    settle(v.r_in.at[some], v.r_out.at[some], v.rt_send)
    settle(v.r_out.at[some], v.r_all.at[some], v.rb_send)
    settle(v.e2_out.at[most], v.e2_in.at[most], v.e2_send)
    settle(v.a_out.at[some], v.a_all.at[some], v.ab_send)

    @pl.when(combiner != node)
    def _():
        settle(v.e2_out.at[0], v.e2_in.at[0], v.e2_own)


def local(nodes, span, iterate, start_field, spanwise_velocity, eigen_basis, inverse_basis, decay_rates):
    ny, modes = iterate.shape[2], iterate.shape[3]
    lines = spanwise_velocity.shape[1]
    share, rows = span // nodes, ny // nodes
    quadrature, shifts = collocation(nodes)
    mats, turns = tables(span, modes, lines)
    operands = [
        jnp.swapaxes(iterate[0], 1, 2),
        jnp.swapaxes(start_field, 1, 2),
        spanwise_velocity.reshape(-1, LANES),
        eigen_basis,
        inverse_basis,
        decay_rates[None],
        jnp.asarray(mats),
        jnp.asarray(turns),
    ]
    sizes = dict(
        nodes=nodes, span=span, lines=lines, modes=modes, ny=ny, nz=span * modes, share=share,
        rows=rows, group=math.gcd(16, span), chunk_rows=HALF // 4,
        quadrature=quadrature, shifts=shifts,
    )
    dma = pltpu.SemaphoreType.DMA
    square = pltpu.VMEM((ny, ny), BF)
    field = pltpu.VMEM((ny, LANES), F32)
    wide = pltpu.VMEM((LANES, lines * LANES), F32)
    lines_bf = pltpu.VMEM((span, 8, LANES), BF)
    parts_f32 = pltpu.VMEM((nodes, rows, LANES), F32)
    parts_bf = pltpu.VMEM((nodes, share, 8, LANES), BF)
    scratch = {name: pltpu.VMEM(x.shape, x.dtype) for name, x in zip(INPUTS, operands, strict=True)}
    scratch |= dict(
        fields_t=pltpu.VMEM((LANES, ny), F32), fields=field, damping=field,
        inv_hi=square, inv_lo=square, eig_hi=square, eig_lo=square,
        velocity=wide, coeff=pltpu.VMEM((ny, 2 * LANES), F32), base=field, inverse_den=field,
        lines_f32=pltpu.VMEM((span, 8, LANES), F32), e1_out=lines_bf, e1_in=lines_bf,
        r_in=parts_f32, r_out=parts_f32, r_all=parts_f32,
        e2_out=lines_bf, e2_in=lines_bf, a_out=parts_bf, a_all=parts_bf,
        load=dma((len(INPUTS),)),
        e1_send=dma, e1_recv=dma, rt_send=dma, rt_recv=dma, rb_send=dma, rb_recv=dma,
        e2_send=dma, e2_own=dma, e2_recv=dma, ab_send=dma, ab_recv=dma,
    )
    updated = pl.pallas_call(
        functools.partial(sweep, sizes, tuple(scratch)),
        out_shape=jax.ShapeDtypeStruct((2, modes, ny), F32),
        in_specs=[pl.BlockSpec(memory_space=pltpu.HBM)] * len(INPUTS),
        out_specs=pl.BlockSpec(memory_space=pltpu.VMEM),
        scratch_shapes=list(scratch.values()),
        compiler_params=pltpu.CompilerParams(
            collective_id=0, has_side_effects=True, vmem_limit_bytes=60 << 20
        ),
    )(*operands)
    return jnp.swapaxes(updated, 1, 2)[None]


def solution(mesh):
    return jax.shard_map(
        functools.partial(local, mesh.shape["node"], mesh.shape["span"]),
        mesh=mesh,
        in_specs=(
            P("node", None, None, "span"),
            P(None, None, "span"),
            P("node", "span", None),
            P(),
            P(),
            P(),
        ),
        out_specs=P("node", None, None, "span"),
        check_vma=False,
    )
```

```python
import functools
import math
from types import SimpleNamespace

import jax
import jax.numpy as jnp
import ml_dtypes
import numpy as np
from jax import lax
from jax.experimental import pallas as pl
from jax.experimental.pallas import tpu as pltpu
from jax.sharding import PartitionSpec as P

MESH = pl.DeviceIdType.MESH
BF = jnp.bfloat16
F32 = jnp.float32
HALF = 64
RING = 12
LANES = 128


def collocation(node_total):
    points = [
        0.5 - 0.5 * math.cos((2.0 * m + 1.0) * math.pi / (2.0 * node_total))
        for m in range(node_total)
    ]
    weights = [[0.0] * node_total for _ in range(node_total)]
    for column in range(node_total):
        coeffs = [1.0]
        scale = 1.0
        for other in range(node_total):
            if other != column:
                grown = [0.0] * (len(coeffs) + 1)
                for power in range(len(coeffs)):
                    grown[power + 1] += coeffs[power]
                    grown[power] -= points[other] * coeffs[power]
                coeffs = grown
                scale = scale * (points[column] - points[other])
        for row in range(node_total):
            total = 0.0
            for power in range(len(coeffs)):
                total += coeffs[power] * points[row] ** (power + 1) / (power + 1)
            weights[row][column] = total / scale
    return (weights, [value / node_total for value in points])


def split_np(table):
    high = table.astype(np.float32).astype(ml_dtypes.bfloat16)
    low = (table - high.astype(np.float64)).astype(ml_dtypes.bfloat16)
    return high, low


def tables(span, local_modes, lines):
    nz = span * local_modes
    s = np.arange(span, dtype=np.int64)
    r = np.arange(local_modes, dtype=np.int64)
    outer = 2 * np.pi * ((s[:, None] * s[None, :]) % span) / span
    inner = 2 * np.pi * ((r[:, None] * r[None, :]) % local_modes) / local_modes
    twist = 2 * np.pi * (s[:, None] * r[None, :]) / nz
    first = np.zeros((LANES, 2 * span))
    first[:span, :span] = np.cos(outer)
    first[:span, span:] = np.sin(outer)
    last = np.zeros((LANES, 2 * LANES))
    last[:span, :span] = np.cos(outer)
    last[:span, LANES : LANES + span] = np.sin(outer)

    place = (r % 4) * (HALF // 4) + r // 4

    def complex_block(phase, rows, columns):
        block = np.zeros((LANES, LANES))
        for i, row_half in enumerate((0, HALF)):
            for j, column_half in enumerate((0, HALF)):
                value = np.cos(phase) if i == j else (np.sin(phase) if i else -np.sin(phase))
                block[np.ix_(rows + row_half, columns + column_half)] = value
        return block

    to_points = complex_block(inner.T, place, r)
    to_modes = complex_block(-inner, r, place)
    cosine, sine = np.zeros((LANES, LANES)), np.zeros((LANES, LANES))
    cosine[:span, :local_modes] = np.cos(twist)
    cosine[:span, HALF : HALF + local_modes] = np.cos(twist)
    sine[:span, :local_modes] = -np.sin(twist)
    sine[:span, HALF : HALF + local_modes] = np.sin(twist)
    turns = np.concatenate([cosine, sine, cosine.T, -sine.T], axis=1).astype(np.float32)
    group = math.gcd(16, span)
    spread = np.zeros((LANES, 2 * LANES))
    for g in range(group):
        for y in range(lines):
            spread[g * 8 + y, g * lines + y] = 1.0
            spread[g * lines + y, LANES + g * 8 + y] = 1.0
    width = 2 * LANES

    def wide(a):
        out = np.zeros((LANES, width), ml_dtypes.bfloat16)
        out[:, : a.shape[1]] = a
        return out

    parts = []
    for table in (first, last):
        parts += [wide(t) for t in split_np(table)]
    for table in (to_points, to_modes):
        parts.append(np.concatenate(split_np(table), axis=1))
    parts.append(wide(spread.astype(ml_dtypes.bfloat16)))
    return np.concatenate(parts, axis=0), turns


def dot(a, b):
    return jnp.dot(a, b, preferred_element_type=F32)


def dot_t(a, b):
    return lax.dot_general(a, b, (((1,), (1,)), ((), ())), preferred_element_type=F32)


def split(x):
    high = x.astype(BF)
    return high, (x - high.astype(F32)).astype(BF)


def three(product, a, b):
    return product(a[0], b[0]) + (product(a[0], b[1]) + product(a[1], b[0]))


def turned(x):
    return pltpu.roll(x, HALF, axis=1)


def greet(barrier, where):
    pl.semaphore_signal(barrier, 1, device_id=where, device_id_type=MESH)


def greeted(barrier, count):
    pl.semaphore_wait(barrier, count)


def remote(source, target, send_sem, recv_sem, where):
    return pltpu.make_async_remote_copy(
        src_ref=source, dst_ref=target, send_sem=send_sem, recv_sem=recv_sem,
        device_id=where, device_id_type=MESH,
    )


def start(copy):
    copy.start()


def settle(source, target, sem):
    pltpu.make_async_copy(source, target, sem).wait()


def prepare_lines(c, v):
    v.fields_t[...] = jnp.zeros_like(v.fields_t)
    v.fields_t[0 : c.modes] = v.iterate[0]
    v.fields_t[HALF : HALF + c.modes] = v.iterate[1]
    v.fields[...] = v.fields_t[...].T
    gradient = (turned(v.fields[...]) * (c.signed * c.turn_sign)).astype(BF)
    spread = v.mats[pl.ds(6 * LANES, c.group * 8), : c.group * c.lines]
    for g in range(c.span // c.group):
        step = c.group * c.lines
        block = dot(spread, gradient[g * step : (g + 1) * step])
        v.e1_out[pl.ds(g * c.group, c.group)] = block.reshape(c.group, 8, LANES).astype(BF)


def prepare_rest(c, v):
    v.fields_t[0 : c.modes] = v.start_field[0]
    v.fields_t[HALF : HALF + c.modes] = v.start_field[1]
    high, low = split(v.inv[...])
    v.inv_hi[...] = high
    v.inv_lo[...] = low
    high, low = split(v.eig[...])
    v.eig_hi[...] = high
    v.eig_lo[...] = low
    both = jnp.concatenate([v.fields[...], v.fields_t[...].T], axis=1)
    v.coeff[...] = three(dot, (v.inv_hi[...], v.inv_lo[...]), split(both))
    v.damping[...] = jnp.broadcast_to(v.rate[...], (LANES, c.ny)).T + c.signed * c.signed
    v.velocity[...] = jnp.zeros_like(v.velocity)
    for y in range(c.lines):
        for k, part in enumerate(velocity_rows(c, v, y)):
            part = part * (-1.0 / c.nz)
            for half in (0, HALF):
                at = half + k * c.chunk_rows
                v.velocity[at : at + part.shape[0], y * LANES : (y + 1) * LANES] = part
    v.lines_f32[...] = jnp.zeros_like(v.lines_f32)


def velocity_rows(c, v, y):
    count = c.modes // 4
    rows = [v.velocity_in[pl.ds(y * count * 3 + i, count, stride=3), :] for i in range(3)]
    lane = lax.broadcasted_iota(jnp.int32, (1, LANES), 1)

    def rolled(i, by):
        return pltpu.roll(rows[i], by, axis=1)

    return (
        rows[0],
        jnp.where(lane < 32, rolled(0, 32), rolled(1, 32)),
        jnp.where(lane < 64, rolled(1, 64), rolled(2, 64)),
        rolled(2, 96),
    )


def mix(c, terms, m):
    total = terms[0] * c.quadrature[m][0]
    for j in range(1, c.nodes):
        total = total + terms[j] * c.quadrature[m][j]
    return total


def blend_fields(c, v):
    def step(i, carry):
        at = pl.ds(pl.multiple_of(i * 8, 8), 8)
        terms = [v.r_in[j, at] for j in range(c.nodes)]
        for m in range(c.nodes):
            v.r_out[m, at] = mix(c, terms, m)
        return carry

    lax.fori_loop(0, c.rows // 8, step, 0)


def blend_modes(c, v):
    def step(i, carry):
        terms = [v.e2_in[j * c.share + i].astype(F32) for j in range(c.nodes)]
        for m in range(c.nodes):
            v.a_out[m, i] = mix(c, terms, m).astype(BF)
        return carry

    lax.fori_loop(0, c.share, step, 0)


def transform(c, v):
    v.lines_f32[...] = v.e1_in[...].astype(F32)
    columns = [v.lines_f32[:, y, :] for y in range(c.lines)]
    stacked = jnp.concatenate(
        [
            jnp.concatenate(columns, axis=1),
            jnp.concatenate([turned(x) * c.turn_sign for x in columns], axis=1),
        ],
        axis=0,
    ).astype(BF)
    first = [v.mats[pl.ds(i * LANES, LANES), : 2 * c.span] for i in (0, 1)]
    grid = dot(first[0], stacked) + dot(first[1], stacked)
    cosine, sine = v.turns[:, 0:LANES], v.turns[:, LANES : 2 * LANES]
    pieces = []
    for y in range(c.lines):
        piece = grid[:, y * LANES : (y + 1) * LANES]
        pieces.append(piece * cosine + turned(piece) * sine)
    tall = split(jnp.concatenate(pieces, axis=0))
    to_points = [v.mats[pl.ds(4 * LANES, LANES), i * LANES : (i + 1) * LANES] for i in (0, 1)]
    to_modes = [v.mats[pl.ds(5 * LANES, LANES), i * LANES : (i + 1) * LANES] for i in (0, 1)]
    physical = three(dot_t, to_points, tall)
    modes = three(dot, to_modes, split(physical * v.velocity[...]))
    swapped = jnp.concatenate([modes[HALF:], modes[:HALF]], axis=0)
    cosine, sine = v.turns[:, 2 * LANES : 3 * LANES], v.turns[:, 3 * LANES : 4 * LANES]
    pieces = []
    for y in range(c.lines):
        at = slice(y * LANES, (y + 1) * LANES)
        piece = modes[:, at] * cosine + swapped[:, at] * sine
        other = jnp.concatenate([piece[HALF:], -piece[:HALF]], axis=0)
        pieces.append(jnp.concatenate([piece, other], axis=1))
    tall = split(jnp.concatenate(pieces, axis=0))
    last = [v.mats[pl.ds(i * LANES, c.span), :] for i in (2, 3)]
    spectral = three(dot_t, last, tall)
    for y in range(c.lines):
        v.lines_f32[:, y, :] = spectral[:, y * LANES : (y + 1) * LANES]
    v.e2_out[...] = v.lines_f32[...].astype(BF)


def known_part(c, v):
    weighted = three(
        dot, (v.inv_hi[...], v.inv_lo[...]), split(v.r_all[...].reshape(c.ny, LANES))
    )
    damping = v.damping[...]
    v.inverse_den[...] = 1.0 / (1.0 + c.shift * damping)
    known = v.coeff[:, LANES:] - damping * weighted + (c.shift * damping) * v.coeff[:, :LANES]
    v.base[...] = three(dot, (v.eig_hi[...], v.eig_lo[...]), split(known * v.inverse_den[...]))


def finish(c, v, out_ref):
    gather = v.mats[pl.ds(6 * LANES, c.group * c.lines), LANES : LANES + c.group * 8]
    arrived = v.a_all[...].astype(F32).reshape(c.span * 8, LANES).astype(BF)
    terms = []
    for g in range(c.span // c.group):
        terms.append(dot(gather, arrived[g * c.group * 8 : (g + 1) * c.group * 8]))
    term = jnp.concatenate(terms, axis=0).astype(BF)
    projected = dot(v.inv_hi[...], term) + dot(v.inv_lo[...], term)
    result = v.base[...] + three(
        dot, (v.eig_hi[...], v.eig_lo[...]), split(projected * v.inverse_den[...])
    )
    result = result.T
    out_ref[0] = result[0 : c.modes]
    out_ref[1] = result[HALF : HALF + c.modes]


INPUTS = ("iterate", "start_field", "velocity_in", "eig", "inv", "rate", "mats", "turns")


def sweep(sizes, names, *refs):
    c = SimpleNamespace(**sizes)
    count = len(INPUTS)
    sources, out_ref = refs[:count], refs[count]
    v = SimpleNamespace(**dict(zip(names, refs[count + 1 :], strict=True)))
    nodes, span = c.nodes, c.span
    node, me = lax.axis_index("node"), lax.axis_index("span")

    def each_peer(act):
        chips, runs = c.chips, span // (2 * c.chips)
        run, chip, core = me // (2 * chips), lax.rem(me // 2, chips), lax.rem(me, 2)

        def ring(chip, others):
            for d in range(runs - 1, -1, -1):
                for e in (1, 0):
                    if others or d or e:
                        other = lax.rem(run + d, runs) * chips + chip
                        act(other * 2 + lax.rem(core + e, 2))

        def step(i, carry):
            away = chips // 2 + ((i + 1) // 2) * (1 - 2 * lax.rem(i, 2))
            ring(lax.rem(chip + away, chips), True)
            return carry

        lax.fori_loop(0, chips - 1, step, 0)
        ring(chip, False)

    barrier = pltpu.get_barrier_semaphore()
    each_peer(lambda peer: greet(barrier, {"span": peer}))
    for k in range(1, nodes):
        greet(barrier, {"node": lax.rem(node + k, nodes)})

    loads = {
        name: pltpu.make_async_copy(source, getattr(v, name), v.load.at[i])
        for i, (name, source) in enumerate(zip(INPUTS, sources, strict=True))
    }
    order = ("iterate", "mats", "inv", "start_field", "eig", "velocity_in", "rate", "turns")
    for name in order:
        loads[name].start()

    lane = lax.broadcasted_iota(jnp.int32, (1, LANES), 1)
    mode = me * c.modes + lax.rem(lane, HALF)
    c.signed = jnp.where(mode < c.nz // 2, mode, mode - c.nz).astype(F32) / (c.nz // 2)
    c.turn_sign = jnp.where(lane < HALF, -1.0, 1.0).astype(F32)
    c.shift = jnp.float32(0.0)
    for m in range(nodes):
        c.shift = jnp.where(node == m, jnp.float32(c.shifts[m]), c.shift)
    for name in order[:2]:
        loads[name].wait()
    prepare_lines(c, v)
    for name in order[2:]:
        loads[name].wait()
    prepare_rest(c, v)
    greeted(barrier, span - 1 + nodes - 1)
    for k in range(1, nodes):
        greet(v.ready, {"node": lax.rem(node + k, nodes)})

    def send_lines(peer):
        start(remote(v.e1_out.at[peer], v.e1_in.at[me], v.e1_send, v.e1_recv, {"span": peer}))

    each_peer(send_lines)

    def to_nodes(source, target, send_sem, recv_sem):
        for k in range(1, nodes):
            peer = lax.rem(node + k, nodes)
            start(remote(source(peer), target, send_sem, recv_sem, {"node": peer}))

    def part(owner):
        return pl.ds(pl.multiple_of(owner * c.rows, 8), c.rows)

    to_nodes(lambda peer: v.fields.at[part(peer)], v.r_in.at[node], v.rt_send, v.rt_recv)
    v.e1_in[me] = v.e1_out[me]
    v.r_in[node] = v.fields[part(node)]
    some, most = pl.ds(0, nodes - 1), pl.ds(0, span - 1)

    settle(v.e1_out.at[most], v.e1_in.at[most], v.e1_recv)
    transform(c, v)

    greeted(v.ready, nodes - 1)
    combiner = me // c.share
    slot = node * c.share + lax.rem(me, c.share)

    def send_modes(peer):
        where = {"node": combiner, "span": peer}
        start(remote(v.e2_out.at[peer], v.e2_in.at[slot], v.e2_send, v.e2_recv, where))

    each_peer(send_modes)
    own = remote(v.e2_out.at[me], v.e2_in.at[slot], v.e2_own, v.e2_recv, {"node": combiner})

    @pl.when(combiner != node)
    def _():
        start(own)

    @pl.when(combiner == node)
    def _():
        start(pltpu.make_async_copy(v.e2_out.at[me], v.e2_in.at[slot], v.e2_recv))

    settle(v.r_in.at[some], v.r_out.at[some], v.rt_recv)
    blend_fields(c, v)
    to_nodes(lambda peer: v.r_out.at[peer], v.r_all.at[node], v.rb_send, v.rb_recv)
    v.r_all[node] = v.r_out[node]

    settle(v.e2_out, v.e2_in, v.e2_recv)
    blend_modes(c, v)
    to_nodes(lambda peer: v.a_out.at[peer], v.a_all.at[node], v.ab_send, v.ab_recv)
    v.a_all[node] = v.a_out[node]
    settle(v.r_out.at[some], v.r_all.at[some], v.rb_recv)
    known_part(c, v)
    settle(v.a_out.at[some], v.a_all.at[some], v.ab_recv)
    finish(c, v, out_ref)

    settle(v.e1_out.at[most], v.e1_in.at[most], v.e1_send)
    settle(v.r_in.at[some], v.r_out.at[some], v.rt_send)
    settle(v.r_out.at[some], v.r_all.at[some], v.rb_send)
    settle(v.e2_out.at[most], v.e2_in.at[most], v.e2_send)
    settle(v.a_out.at[some], v.a_all.at[some], v.ab_send)

    @pl.when(combiner != node)
    def _():
        settle(v.e2_out.at[0], v.e2_in.at[0], v.e2_own)


def local(nodes, span, chips, iterate, start_field, spanwise_velocity, eigen_basis, inverse_basis, decay_rates):
    ny, modes = iterate.shape[2], iterate.shape[3]
    lines = spanwise_velocity.shape[1]
    share, rows = span // nodes, ny // nodes
    quadrature, shifts = collocation(nodes)
    mats, turns = tables(span, modes, lines)
    operands = [
        jnp.swapaxes(iterate[0], 1, 2),
        jnp.swapaxes(start_field, 1, 2),
        spanwise_velocity.reshape(-1, LANES),
        eigen_basis,
        inverse_basis,
        decay_rates[None],
        jnp.asarray(mats),
        jnp.asarray(turns),
    ]
    sizes = dict(
        nodes=nodes, span=span, chips=chips, lines=lines, modes=modes, ny=ny, nz=span * modes, share=share,
        rows=rows, group=math.gcd(16, span), chunk_rows=HALF // 4,
        quadrature=quadrature, shifts=shifts,
    )
    dma = pltpu.SemaphoreType.DMA
    square = pltpu.VMEM((ny, ny), BF)
    field = pltpu.VMEM((ny, LANES), F32)
    wide = pltpu.VMEM((LANES, lines * LANES), F32)
    lines_bf = pltpu.VMEM((span, 8, LANES), BF)
    parts_f32 = pltpu.VMEM((nodes, rows, LANES), F32)
    parts_bf = pltpu.VMEM((nodes, share, 8, LANES), BF)
    scratch = {name: pltpu.VMEM(x.shape, x.dtype) for name, x in zip(INPUTS, operands, strict=True)}
    scratch |= dict(
        fields_t=pltpu.VMEM((LANES, ny), F32), fields=field, damping=field,
        inv_hi=square, inv_lo=square, eig_hi=square, eig_lo=square,
        velocity=wide, coeff=pltpu.VMEM((ny, 2 * LANES), F32), base=field, inverse_den=field,
        lines_f32=pltpu.VMEM((span, 8, LANES), F32), e1_out=lines_bf, e1_in=lines_bf,
        r_in=parts_f32, r_out=parts_f32, r_all=parts_f32,
        e2_out=lines_bf, e2_in=lines_bf, a_out=parts_bf, a_all=parts_bf,
        load=dma((len(INPUTS),)), ready=pltpu.SemaphoreType.REGULAR,
        e1_send=dma, e1_recv=dma, rt_send=dma, rt_recv=dma, rb_send=dma, rb_recv=dma,
        e2_send=dma, e2_own=dma, e2_recv=dma, ab_send=dma, ab_recv=dma,
    )
    updated = pl.pallas_call(
        functools.partial(sweep, sizes, tuple(scratch)),
        out_shape=jax.ShapeDtypeStruct((2, modes, ny), F32),
        in_specs=[pl.BlockSpec(memory_space=pltpu.HBM)] * len(INPUTS),
        out_specs=pl.BlockSpec(memory_space=pltpu.VMEM),
        scratch_shapes=list(scratch.values()),
        compiler_params=pltpu.CompilerParams(
            collective_id=0, has_side_effects=True, vmem_limit_bytes=60 << 20
        ),
    )(*operands)
    return jnp.swapaxes(updated, 1, 2)[None]


def solution(mesh):
    return jax.shard_map(
        functools.partial(local, mesh.shape["node"], mesh.shape["span"], RING),
        mesh=mesh,
        in_specs=(
            P("node", None, None, "span"),
            P(None, None, "span"),
            P("node", "span", None),
            P(),
            P(),
            P(),
        ),
        out_specs=P("node", None, None, "span"),
        check_vma=False,
    )
```

```python
import functools
import math
from types import SimpleNamespace

import jax
import jax.numpy as jnp
import ml_dtypes
import numpy as np
from jax import lax
from jax.experimental import pallas as pl
from jax.experimental.pallas import tpu as pltpu
from jax.sharding import PartitionSpec as P

MESH = pl.DeviceIdType.MESH
BF = jnp.bfloat16
F32 = jnp.float32
HALF = 64
RING = 12
LANES = 128


def collocation(node_total):
    points = [
        0.5 - 0.5 * math.cos((2.0 * m + 1.0) * math.pi / (2.0 * node_total))
        for m in range(node_total)
    ]
    weights = [[0.0] * node_total for _ in range(node_total)]
    for column in range(node_total):
        coeffs = [1.0]
        scale = 1.0
        for other in range(node_total):
            if other != column:
                grown = [0.0] * (len(coeffs) + 1)
                for power in range(len(coeffs)):
                    grown[power + 1] += coeffs[power]
                    grown[power] -= points[other] * coeffs[power]
                coeffs = grown
                scale = scale * (points[column] - points[other])
        for row in range(node_total):
            total = 0.0
            for power in range(len(coeffs)):
                total += coeffs[power] * points[row] ** (power + 1) / (power + 1)
            weights[row][column] = total / scale
    return (weights, [value / node_total for value in points])


def split_np(table):
    high = table.astype(np.float32).astype(ml_dtypes.bfloat16)
    low = (table - high.astype(np.float64)).astype(ml_dtypes.bfloat16)
    return high, low


def tables(span, local_modes, lines):
    nz = span * local_modes
    s = np.arange(span, dtype=np.int64)
    r = np.arange(local_modes, dtype=np.int64)
    outer = 2 * np.pi * ((s[:, None] * s[None, :]) % span) / span
    inner = 2 * np.pi * ((r[:, None] * r[None, :]) % local_modes) / local_modes
    twist = 2 * np.pi * (s[:, None] * r[None, :]) / nz
    first = np.zeros((LANES, 2 * span))
    first[:span, :span] = np.cos(outer)
    first[:span, span:] = np.sin(outer)
    last = np.zeros((LANES, 2 * LANES))
    last[:span, :span] = np.cos(outer)
    last[:span, LANES : LANES + span] = np.sin(outer)

    place = (r % 4) * (HALF // 4) + r // 4

    def complex_block(phase, rows, columns):
        block = np.zeros((LANES, LANES))
        for i, row_half in enumerate((0, HALF)):
            for j, column_half in enumerate((0, HALF)):
                value = np.cos(phase) if i == j else (np.sin(phase) if i else -np.sin(phase))
                block[np.ix_(rows + row_half, columns + column_half)] = value
        return block

    to_points = complex_block(inner.T, place, r)
    to_modes = complex_block(-inner, r, place)
    cosine, sine = np.zeros((LANES, LANES)), np.zeros((LANES, LANES))
    cosine[:span, :local_modes] = np.cos(twist)
    cosine[:span, HALF : HALF + local_modes] = np.cos(twist)
    sine[:span, :local_modes] = -np.sin(twist)
    sine[:span, HALF : HALF + local_modes] = np.sin(twist)
    turns = np.concatenate([cosine, sine, cosine.T, -sine.T], axis=1).astype(np.float32)
    group = math.gcd(16, span)
    spread = np.zeros((LANES, 2 * LANES))
    for g in range(group):
        for y in range(lines):
            spread[g * 8 + y, g * lines + y] = 1.0
            spread[g * lines + y, LANES + g * 8 + y] = 1.0
    width = 2 * LANES

    def wide(a):
        out = np.zeros((LANES, width), ml_dtypes.bfloat16)
        out[:, : a.shape[1]] = a
        return out

    parts = []
    for table in (first, last):
        parts += [wide(t) for t in split_np(table)]
    for table in (to_points, to_modes):
        parts.append(np.concatenate(split_np(table), axis=1))
    parts.append(wide(spread.astype(ml_dtypes.bfloat16)))
    return np.concatenate(parts, axis=0), turns


def dot(a, b):
    return jnp.dot(a, b, preferred_element_type=F32)


def dot_t(a, b):
    return lax.dot_general(a, b, (((1,), (1,)), ((), ())), preferred_element_type=F32)


def split(x):
    high = x.astype(BF)
    return high, (x - high.astype(F32)).astype(BF)


def three(product, a, b):
    return product(a[0], b[0]) + (product(a[0], b[1]) + product(a[1], b[0]))


def turned(x):
    return pltpu.roll(x, HALF, axis=1)


def greet(barrier, where):
    pl.semaphore_signal(barrier, 1, device_id=where, device_id_type=MESH)


def greeted(barrier, count):
    pl.semaphore_wait(barrier, count)


def remote(source, target, send_sem, recv_sem, where):
    return pltpu.make_async_remote_copy(
        src_ref=source, dst_ref=target, send_sem=send_sem, recv_sem=recv_sem,
        device_id=where, device_id_type=MESH,
    )


def start(copy):
    copy.start()


def settle(source, target, sem):
    pltpu.make_async_copy(source, target, sem).wait()


def prepare_lines(c, v):
    v.fields_t[...] = jnp.zeros_like(v.fields_t)
    v.fields_t[0 : c.modes] = v.iterate[0]
    v.fields_t[HALF : HALF + c.modes] = v.iterate[1]
    v.fields[...] = v.fields_t[...].T
    gradient = (turned(v.fields[...]) * (c.signed * c.turn_sign)).astype(BF)
    spread = v.mats[pl.ds(6 * LANES, c.group * 8), : c.group * c.lines]
    for g in range(c.span // c.group):
        step = c.group * c.lines
        block = dot(spread, gradient[g * step : (g + 1) * step])
        v.e1_out[pl.ds(g * c.group, c.group)] = block.reshape(c.group, 8, LANES).astype(BF)


def prepare_rest(c, v):
    v.fields_t[0 : c.modes] = v.start_field[0]
    v.fields_t[HALF : HALF + c.modes] = v.start_field[1]
    high, low = split(v.inv[...])
    v.inv_hi[...] = high
    v.inv_lo[...] = low
    high, low = split(v.eig[...])
    v.eig_hi[...] = high
    v.eig_lo[...] = low
    both = jnp.concatenate([v.fields[...], v.fields_t[...].T], axis=1)
    v.coeff[...] = three(dot, (v.inv_hi[...], v.inv_lo[...]), split(both))
    v.damping[...] = jnp.broadcast_to(v.rate[...], (LANES, c.ny)).T + c.signed * c.signed
    v.velocity[...] = jnp.zeros_like(v.velocity)
    for y in range(c.lines):
        for k, part in enumerate(velocity_rows(c, v, y)):
            part = part * (-1.0 / c.nz)
            for half in (0, HALF):
                at = half + k * c.chunk_rows
                v.velocity[at : at + part.shape[0], y * LANES : (y + 1) * LANES] = part
    v.lines_f32[...] = jnp.zeros_like(v.lines_f32)


def velocity_rows(c, v, y):
    count = c.modes // 4
    rows = [v.velocity_in[pl.ds(y * count * 3 + i, count, stride=3), :] for i in range(3)]
    lane = lax.broadcasted_iota(jnp.int32, (1, LANES), 1)

    def rolled(i, by):
        return pltpu.roll(rows[i], by, axis=1)

    return (
        rows[0],
        jnp.where(lane < 32, rolled(0, 32), rolled(1, 32)),
        jnp.where(lane < 64, rolled(1, 64), rolled(2, 64)),
        rolled(2, 96),
    )


def mix(c, terms, m):
    total = terms[0] * c.quadrature[m][0]
    for j in range(1, c.nodes):
        total = total + terms[j] * c.quadrature[m][j]
    return total


def blend_fields(c, v):
    def step(i, carry):
        at = pl.ds(pl.multiple_of(i * 8, 8), 8)
        terms = [v.r_in[j, at] for j in range(c.nodes)]
        for m in range(c.nodes):
            v.r_out[m, at] = mix(c, terms, m)
        return carry

    lax.fori_loop(0, c.rows // 8, step, 0)


def blend_modes(c, v):
    def step(i, carry):
        terms = [v.e2_in[j * c.share + i].astype(F32) for j in range(c.nodes)]
        for m in range(c.nodes):
            v.a_out[m, i] = mix(c, terms, m).astype(BF)
        return carry

    lax.fori_loop(0, c.share, step, 0)


def transform(c, v):
    v.lines_f32[...] = v.e1_in[...].astype(F32)
    columns = [v.lines_f32[:, y, :] for y in range(c.lines)]
    stacked = jnp.concatenate(
        [
            jnp.concatenate(columns, axis=1),
            jnp.concatenate([turned(x) * c.turn_sign for x in columns], axis=1),
        ],
        axis=0,
    ).astype(BF)
    first = [v.mats[pl.ds(i * LANES, LANES), : 2 * c.span] for i in (0, 1)]
    grid = dot(first[0], stacked) + dot(first[1], stacked)
    cosine, sine = v.turns[:, 0:LANES], v.turns[:, LANES : 2 * LANES]
    pieces = []
    for y in range(c.lines):
        piece = grid[:, y * LANES : (y + 1) * LANES]
        pieces.append(piece * cosine + turned(piece) * sine)
    tall = split(jnp.concatenate(pieces, axis=0))
    to_points = [v.mats[pl.ds(4 * LANES, LANES), i * LANES : (i + 1) * LANES] for i in (0, 1)]
    to_modes = [v.mats[pl.ds(5 * LANES, LANES), i * LANES : (i + 1) * LANES] for i in (0, 1)]
    physical = three(dot_t, to_points, tall)
    modes = three(dot, to_modes, split(physical * v.velocity[...]))
    swapped = jnp.concatenate([modes[HALF:], modes[:HALF]], axis=0)
    cosine, sine = v.turns[:, 2 * LANES : 3 * LANES], v.turns[:, 3 * LANES : 4 * LANES]
    pieces = []
    for y in range(c.lines):
        at = slice(y * LANES, (y + 1) * LANES)
        piece = modes[:, at] * cosine + swapped[:, at] * sine
        other = jnp.concatenate([piece[HALF:], -piece[:HALF]], axis=0)
        pieces.append(jnp.concatenate([piece, other], axis=1))
    tall = split(jnp.concatenate(pieces, axis=0))
    last = [v.mats[pl.ds(i * LANES, c.span), :] for i in (2, 3)]
    spectral = three(dot_t, last, tall)
    for y in range(c.lines):
        v.lines_f32[:, y, :] = spectral[:, y * LANES : (y + 1) * LANES]
    v.e2_out[...] = v.lines_f32[...].astype(BF)


def known_part(c, v):
    weighted = three(
        dot, (v.inv_hi[...], v.inv_lo[...]), split(v.r_all[...].reshape(c.ny, LANES))
    )
    damping = v.damping[...]
    v.inverse_den[...] = 1.0 / (1.0 + c.shift * damping)
    known = v.coeff[:, LANES:] - damping * weighted + (c.shift * damping) * v.coeff[:, :LANES]
    v.base[...] = three(dot, (v.eig_hi[...], v.eig_lo[...]), split(known * v.inverse_den[...]))


def finish(c, v, out_ref):
    gather = v.mats[pl.ds(6 * LANES, c.group * c.lines), LANES : LANES + c.group * 8]
    arrived = v.a_all[...].astype(F32).reshape(c.span * 8, LANES).astype(BF)
    terms = []
    for g in range(c.span // c.group):
        terms.append(dot(gather, arrived[g * c.group * 8 : (g + 1) * c.group * 8]))
    term = jnp.concatenate(terms, axis=0).astype(BF)
    projected = dot(v.inv_hi[...], term) + dot(v.inv_lo[...], term)
    result = v.base[...] + three(
        dot, (v.eig_hi[...], v.eig_lo[...]), split(projected * v.inverse_den[...])
    )
    result = result.T
    out_ref[0] = result[0 : c.modes]
    out_ref[1] = result[HALF : HALF + c.modes]


INPUTS = ("iterate", "start_field", "velocity_in", "eig", "inv", "rate", "mats", "turns")


def sweep(sizes, names, *refs):
    c = SimpleNamespace(**sizes)
    count = len(INPUTS)
    sources, out_ref = refs[:count], refs[count]
    v = SimpleNamespace(**dict(zip(names, refs[count + 1 :], strict=True)))
    nodes, span = c.nodes, c.span
    node, me = lax.axis_index("node"), lax.axis_index("span")

    def each_peer(act):
        chips, runs = c.chips, span // (2 * c.chips)
        run, chip, core = me // (2 * chips), lax.rem(me // 2, chips), lax.rem(me, 2)

        def ring(chip, others):
            for d in range(runs - 1, -1, -1):
                for e in (1, 0):
                    if others or d or e:
                        other = lax.rem(run + d, runs) * chips + chip
                        act(other * 2 + lax.rem(core + e, 2))

        def step(i, carry):
            away = chips // 2 + ((i + 1) // 2) * (1 - 2 * lax.rem(i, 2))
            ring(lax.rem(chip + away, chips), True)
            return carry

        lax.fori_loop(0, chips - 1, step, 0)
        ring(chip, False)

    def each_neighbour(act):
        def step(k, carry):
            act(lax.rem(me + k, span))
            return carry

        lax.fori_loop(1, span, step, 0)

    barrier = pltpu.get_barrier_semaphore()
    each_neighbour(lambda peer: greet(barrier, {"span": peer}))
    for k in range(1, nodes):
        greet(barrier, {"node": lax.rem(node + k, nodes)})

    loads = {
        name: pltpu.make_async_copy(source, getattr(v, name), v.load.at[i])
        for i, (name, source) in enumerate(zip(INPUTS, sources, strict=True))
    }
    order = ("iterate", "mats", "inv", "start_field", "eig", "velocity_in", "rate", "turns")
    for name in order:
        loads[name].start()

    lane = lax.broadcasted_iota(jnp.int32, (1, LANES), 1)
    mode = me * c.modes + lax.rem(lane, HALF)
    c.signed = jnp.where(mode < c.nz // 2, mode, mode - c.nz).astype(F32) / (c.nz // 2)
    c.turn_sign = jnp.where(lane < HALF, -1.0, 1.0).astype(F32)
    c.shift = jnp.float32(0.0)
    for m in range(nodes):
        c.shift = jnp.where(node == m, jnp.float32(c.shifts[m]), c.shift)
    for name in order[:2]:
        loads[name].wait()
    prepare_lines(c, v)
    for name in order[2:]:
        loads[name].wait()
    prepare_rest(c, v)
    greeted(barrier, span - 1 + nodes - 1)
    for k in range(1, nodes):
        greet(v.ready, {"node": lax.rem(node + k, nodes)})

    def send_lines(peer):
        start(remote(v.e1_out.at[peer], v.e1_in.at[me], v.e1_send, v.e1_recv, {"span": peer}))

    each_neighbour(send_lines)

    def to_nodes(source, target, send_sem, recv_sem):
        for k in range(1, nodes):
            peer = lax.rem(node + k, nodes)
            start(remote(source(peer), target, send_sem, recv_sem, {"node": peer}))

    def part(owner):
        return pl.ds(pl.multiple_of(owner * c.rows, 8), c.rows)

    to_nodes(lambda peer: v.fields.at[part(peer)], v.r_in.at[node], v.rt_send, v.rt_recv)
    v.e1_in[me] = v.e1_out[me]
    v.r_in[node] = v.fields[part(node)]
    some, most = pl.ds(0, nodes - 1), pl.ds(0, span - 1)

    settle(v.e1_out.at[most], v.e1_in.at[most], v.e1_recv)
    transform(c, v)

    greeted(v.ready, nodes - 1)
    combiner = me // c.share
    slot = node * c.share + lax.rem(me, c.share)

    def send_modes(peer):
        where = {"node": combiner, "span": peer}
        start(remote(v.e2_out.at[peer], v.e2_in.at[slot], v.e2_send, v.e2_recv, where))

    each_peer(send_modes)
    own = remote(v.e2_out.at[me], v.e2_in.at[slot], v.e2_own, v.e2_recv, {"node": combiner})

    @pl.when(combiner != node)
    def _():
        start(own)

    @pl.when(combiner == node)
    def _():
        start(pltpu.make_async_copy(v.e2_out.at[me], v.e2_in.at[slot], v.e2_recv))

    settle(v.r_in.at[some], v.r_out.at[some], v.rt_recv)
    blend_fields(c, v)
    to_nodes(lambda peer: v.r_out.at[peer], v.r_all.at[node], v.rb_send, v.rb_recv)
    v.r_all[node] = v.r_out[node]

    settle(v.e2_out, v.e2_in, v.e2_recv)
    blend_modes(c, v)
    to_nodes(lambda peer: v.a_out.at[peer], v.a_all.at[node], v.ab_send, v.ab_recv)
    v.a_all[node] = v.a_out[node]
    settle(v.r_out.at[some], v.r_all.at[some], v.rb_recv)
    known_part(c, v)
    settle(v.a_out.at[some], v.a_all.at[some], v.ab_recv)
    finish(c, v, out_ref)

    settle(v.e1_out.at[most], v.e1_in.at[most], v.e1_send)
    settle(v.r_in.at[some], v.r_out.at[some], v.rt_send)
    settle(v.r_out.at[some], v.r_all.at[some], v.rb_send)
    settle(v.e2_out.at[most], v.e2_in.at[most], v.e2_send)
    settle(v.a_out.at[some], v.a_all.at[some], v.ab_send)

    @pl.when(combiner != node)
    def _():
        settle(v.e2_out.at[0], v.e2_in.at[0], v.e2_own)


def local(nodes, span, chips, iterate, start_field, spanwise_velocity, eigen_basis, inverse_basis, decay_rates):
    ny, modes = iterate.shape[2], iterate.shape[3]
    lines = spanwise_velocity.shape[1]
    share, rows = span // nodes, ny // nodes
    quadrature, shifts = collocation(nodes)
    mats, turns = tables(span, modes, lines)
    operands = [
        jnp.swapaxes(iterate[0], 1, 2),
        jnp.swapaxes(start_field, 1, 2),
        spanwise_velocity.reshape(-1, LANES),
        eigen_basis,
        inverse_basis,
        decay_rates[None],
        jnp.asarray(mats),
        jnp.asarray(turns),
    ]
    sizes = dict(
        nodes=nodes, span=span, chips=chips, lines=lines, modes=modes, ny=ny, nz=span * modes, share=share,
        rows=rows, group=math.gcd(16, span), chunk_rows=HALF // 4,
        quadrature=quadrature, shifts=shifts,
    )
    dma = pltpu.SemaphoreType.DMA
    square = pltpu.VMEM((ny, ny), BF)
    field = pltpu.VMEM((ny, LANES), F32)
    wide = pltpu.VMEM((LANES, lines * LANES), F32)
    lines_bf = pltpu.VMEM((span, 8, LANES), BF)
    parts_f32 = pltpu.VMEM((nodes, rows, LANES), F32)
    parts_bf = pltpu.VMEM((nodes, share, 8, LANES), BF)
    scratch = {name: pltpu.VMEM(x.shape, x.dtype) for name, x in zip(INPUTS, operands, strict=True)}
    scratch |= dict(
        fields_t=pltpu.VMEM((LANES, ny), F32), fields=field, damping=field,
        inv_hi=square, inv_lo=square, eig_hi=square, eig_lo=square,
        velocity=wide, coeff=pltpu.VMEM((ny, 2 * LANES), F32), base=field, inverse_den=field,
        lines_f32=pltpu.VMEM((span, 8, LANES), F32), e1_out=lines_bf, e1_in=lines_bf,
        r_in=parts_f32, r_out=parts_f32, r_all=parts_f32,
        e2_out=lines_bf, e2_in=lines_bf, a_out=parts_bf, a_all=parts_bf,
        load=dma((len(INPUTS),)), ready=pltpu.SemaphoreType.REGULAR,
        e1_send=dma, e1_recv=dma, rt_send=dma, rt_recv=dma, rb_send=dma, rb_recv=dma,
        e2_send=dma, e2_own=dma, e2_recv=dma, ab_send=dma, ab_recv=dma,
    )
    updated = pl.pallas_call(
        functools.partial(sweep, sizes, tuple(scratch)),
        out_shape=jax.ShapeDtypeStruct((2, modes, ny), F32),
        in_specs=[pl.BlockSpec(memory_space=pltpu.HBM)] * len(INPUTS),
        out_specs=pl.BlockSpec(memory_space=pltpu.VMEM),
        scratch_shapes=list(scratch.values()),
        compiler_params=pltpu.CompilerParams(
            collective_id=0, has_side_effects=True, vmem_limit_bytes=60 << 20
        ),
    )(*operands)
    return jnp.swapaxes(updated, 1, 2)[None]


def solution(mesh):
    return jax.shard_map(
        functools.partial(local, mesh.shape["node"], mesh.shape["span"], RING),
        mesh=mesh,
        in_specs=(
            P("node", None, None, "span"),
            P(None, None, "span"),
            P("node", "span", None),
            P(),
            P(),
            P(),
        ),
        out_specs=P("node", None, None, "span"),
        check_vma=False,
    )
```
